32 devices in a mesh: seq: 8 (over z, x), dp: 4 (over y, core).
Axes of the slice: x: 2, y: 2, z: 4, core: 2. Of those that a mesh axis runs over, the one named last changes fastest.
Arguments:
- inputs: bfloat16 [8, 1024, 1024], P('dp', 'seq'), may hold values from -6 to 6
- cotangent: bfloat16 [8, 1024, 1024], P('dp', 'seq'), may hold values from -6 to 6
- attn_gain: bfloat16 [1024], P('seq'), may hold values from 0.099609375 to 1.8984375
- w_query: bfloat16 [1024, 512], P('seq'), may hold values from -0.1875 to 0.1875
- w_key: bfloat16 [1024, 512], P('seq'), may hold values from -0.1875 to 0.1875
- w_value: bfloat16 [1024, 1024], P('seq'), may hold values from -0.1875 to 0.1875
- w_gate: bfloat16 [1024, 1024], P('seq'), may hold values from -0.1875 to 0.1875
- w_rank_in: bfloat16 [1024, 16], P('seq'), may hold values from -0.1875 to 0.1875
- w_rank_out: bfloat16 [16, 512], P('seq'), may hold values from -1.5 to 1.5
- rank_bias: bfloat16 [512], P('seq'), may hold values from 1 to 7
- out_gain: bfloat16 [256], P('seq'), may hold values from 0.099609375 to 1.8984375
- w_out: bfloat16 [1024, 1024], P('seq'), may hold values from -0.375 to 0.375
- mlp_gain: bfloat16 [1024], P('seq'), may hold values from 0.099609375 to 1.8984375
- w_gate_ff: bfloat16 [1024, 2816], P('seq'), may hold values from -0.1875 to 0.1875
- w_up: bfloat16 [1024, 2816], P('seq'), may hold values from -0.1875 to 0.1875
- w_down: bfloat16 [2816, 1024], P('seq'), may hold values from -0.21875 to 0.21875
Outputs:
- output: bfloat16 [8, 1024, 1024], P('dp', 'seq')
- input_grad: bfloat16 [8, 1024, 1024], P('dp', 'seq')
- grad_attn_gain: float32 [1024], P('seq')
- grad_w_query: float32 [1024, 512], P('seq')
- grad_w_key: float32 [1024, 512], P('seq')
- grad_w_value: float32 [1024, 1024], P('seq')
- grad_w_gate: float32 [1024, 1024], P('seq')
- grad_w_rank_in: float32 [1024, 16], P('seq')
- grad_w_rank_out: float32 [16, 512], P('seq')
- grad_rank_bias: float32 [512], P('seq')
- grad_out_gain: float32 [256], P('seq')
- grad_w_out: float32 [1024, 1024], P('seq')
- grad_mlp_gain: float32 [1024], P('seq')
- grad_w_gate_ff: float32 [1024, 2816], P('seq')
- grad_w_up: float32 [1024, 2816], P('seq')
- grad_w_down: float32 [2816, 1024], P('seq')
The draws below stay inside these ranges and needn't reach their ends.
All inputs are finite; a program needn't handle non-finite values.
Results may differ from the reference program's by a relative error of at most 0.03.
Values may be sent and summed in bfloat16 or wider, within the bound.
A program may use at most 192 MiB of HBM per device.

```python
import jax
import jax.numpy as jnp
from jax import lax

D = 1024
HEADS = 4
KH = 128
VH = 256
RANK = 16
FF = 2816
BLOCK = 64
SEQ_LEN = 1024
BATCH = 8
KEYS = 512
VALS = 1024


def shard_levels(key, extent, cuts, smallest, largest):
    level, own = 1.0, jax.random.fold_in(key, 6)
    for axis_at, shards_of in cuts:
        heights = jnp.exp(jax.random.uniform(jax.random.fold_in(own, axis_at), (shards_of,), jnp.float32, smallest / len(cuts), largest / len(cuts)))
        level = level * jnp.repeat(heights, extent[axis_at] // shards_of).reshape([-1 if axis == axis_at else 1 for axis in range(len(extent))])
    return level


def normal_values(own_key, shape, scale, most, cuts=(), kind=jnp.bfloat16):
    array = jax.random.normal(own_key, shape, jnp.float32) * scale
    if len(cuts) > 0:
        array = shard_levels(own_key, shape, cuts, -0.22, 0.18) * array
    return jnp.clip(array, min=-most, max=most).astype(kind)


def setup_inputs(seed: int = 0) -> dict:
    streams_of = jax.random.split(jax.random.key(seed), 17)
    return {
        "inputs": normal_values(streams_of[0], (BATCH, SEQ_LEN, D), 1.0, 6.0, ((0, 4), (1, 8))),
        "cotangent": normal_values(streams_of[1], (BATCH, SEQ_LEN, D), 1.0, 6.0, ((0, 4), (1, 8))),
        "attn_gain": jnp.clip(1.0 + 0.18 * jax.random.normal(streams_of[2], (D,), jnp.float32), 0.099609375, 1.8984375).astype(jnp.bfloat16),
        "w_query": normal_values(streams_of[3], (D, KEYS), D ** -0.5, 0.1875, ((0, 8),)),
        "w_key": normal_values(streams_of[4], (D, KEYS), D ** -0.5, 0.1875, ((0, 8),)),
        "w_value": normal_values(streams_of[5], (D, VALS), D ** -0.5, 0.1875, ((0, 8),)),
        "w_gate": normal_values(streams_of[6], (D, VALS), D ** -0.5, 0.1875, ((0, 8),)),
        "w_rank_in": normal_values(streams_of[7], (D, RANK), D ** -0.5, 0.1875, ((0, 8),)),
        "w_rank_out": normal_values(streams_of[8], (RANK, KEYS), RANK ** -0.5, 1.5, ((0, 8),)),
        "rank_bias": jnp.clip(1.0 + 6.0 * jax.random.uniform(streams_of[9], (KEYS,), jnp.float32) ** shard_levels(streams_of[9], (KEYS,), ((0, 8),), -0.2, 0.2), 1.0, 7.0).astype(jnp.bfloat16),
        "out_gain": jnp.clip(1.0 + 0.18 * jax.random.normal(streams_of[10], (VH,), jnp.float32), 0.099609375, 1.8984375).astype(jnp.bfloat16),
        "w_out": normal_values(streams_of[11], (VALS, D), (VALS // 4) ** -0.5, 0.375, ((0, 8),)),
        "mlp_gain": jnp.clip(1.0 + 0.18 * jax.random.normal(streams_of[12], (D,), jnp.float32), 0.099609375, 1.8984375).astype(jnp.bfloat16),
        "w_gate_ff": normal_values(streams_of[13], (D, FF), D ** -0.5, 0.1875, ((0, 8),)),
        "w_up": normal_values(streams_of[14], (D, FF), D ** -0.5, 0.1875, ((0, 8),)),
        "w_down": normal_values(streams_of[15], (FF, D), (FF // 4) ** -0.5, 0.21875, ((0, 8),)),
    }


EPS = 1e-06
HIGH = lax.Precision.HIGHEST

@jax.custom_vjp
def low(v):
    return lax.optimization_barrier(v.astype(jnp.bfloat16)).astype(jnp.float32)

@jax.custom_vjp
def low_back(v):
    return v

def low_keep(v):
    return (low(v), None)

def low_pass(kept, grad):
    return (grad,)

def back_keep(v):
    return (v, None)

def back_low(kept, grad):
    return (low(grad),)
low.defvjp(low_keep, low_pass)
low_back.defvjp(back_keep, back_low)

def normalize(source, gain):
    return source * lax.rsqrt(lax.optimization_barrier(jnp.mean(source * source, axis=-1, keepdims=True)) + EPS) * gain

def head_normalize(source, gain):
    return source * lax.rsqrt(jnp.maximum(lax.optimization_barrier(jnp.mean(source * source, axis=-1, keepdims=True)), 1.0)) * gain

def project(source, weight):
    return jnp.einsum('bld,df->blf', source, weight, precision=HIGH)

def block_step(memory, pieces):
    queries, key_rows, values, log_decay = pieces
    running = jnp.cumsum(log_decay, axis=2)
    length = running.shape[2]
    target = lax.broadcasted_iota(jnp.int32, (length, length), 0)
    source = lax.broadcasted_iota(jnp.int32, (length, length), 1)
    causal = (target >= source)[:, :, None]
    spread = running[:, :, :, None, :] - running[:, :, None, :, :]
    factor = jnp.exp(jnp.where(causal, spread, 0.0)) * jnp.where(causal, 1.0, 0.0)
    scores = jnp.einsum('bhtk,bhsk,bhtsk->bhts', queries, key_rows, factor, precision=HIGH)
    within = jnp.einsum('bhts,bhsv->bhtv', scores, values, precision=HIGH)
    across = jnp.einsum('bhtk,bhkv->bhtv', queries * jnp.exp(running), memory, precision=HIGH)
    ending = running[:, :, -1:, :]
    carried = jnp.exp(ending - running) * key_rows
    deposit = jnp.einsum('bhsk,bhsv->bhkv', carried, values, precision=HIGH)
    return (jnp.exp(ending[:, :, 0, :])[:, :, :, None] * memory + deposit, within + across)

def to_blocks(source, width):
    batch, length = (source.shape[0], source.shape[1])
    blocked = source.reshape(batch, length // BLOCK, BLOCK, HEADS, width)
    return blocked.transpose(1, 0, 3, 2, 4)

def linear_attention(queries, key_rows, values, log_decay):
    batch, length = (queries.shape[0], queries.shape[1])
    memory = jnp.zeros((batch, HEADS, KH, VH), jnp.float32)
    pieces = (to_blocks(queries, KH), to_blocks(key_rows, KH), to_blocks(values, VH), to_blocks(log_decay, KH))
    ending, blocks_out = lax.scan(jax.checkpoint(block_step), memory, pieces)
    return blocks_out.transpose(1, 0, 3, 2, 4).reshape(batch, length, HEADS, VH)

def layer(inputs, attn_gain, w_query, w_key, w_value, w_gate, w_rank_in, w_rank_out, rank_bias, out_gain, w_out, mlp_gain, w_gate_ff, w_up, w_down):
    batch, length = (inputs.shape[0], inputs.shape[1])
    normed_in = low(normalize(inputs, attn_gain))
    queries = low_back(low(project(normed_in, w_query)))
    key_rows = low_back(low(project(normed_in, w_key)))
    values = low_back(low(project(normed_in, w_value)))
    gate_out = low_back(project(normed_in, w_gate))
    rank_rows = project(normed_in, w_rank_in)
    logits = project(rank_rows, w_rank_out) + rank_bias
    log_decay = jax.nn.log_sigmoid(logits) / 16.0
    mixed = linear_attention(queries * KH ** (-0.5), key_rows, values, log_decay)
    heads_normed = head_normalize(mixed, out_gain).reshape(batch, length, HEADS * VH)
    gated = low(heads_normed * jax.nn.silu(gate_out))
    branch = low_back(project(gated, w_out))
    middle = inputs + branch
    normed_mid = low(normalize(middle, mlp_gain))
    gate_ff = low_back(project(normed_mid, w_gate_ff))
    up_rows = low_back(project(normed_mid, w_up))
    hidden = low(jax.nn.silu(gate_ff) * up_rows)
    return middle + project(hidden, w_down)

def reference(inputs, cotangent, attn_gain, w_query, w_key, w_value, w_gate, w_rank_in, w_rank_out, rank_bias, out_gain, w_out, mlp_gain, w_gate_ff, w_up, w_down):
    weights = (attn_gain, w_query, w_key, w_value, w_gate, w_rank_in, w_rank_out, rank_bias, out_gain, w_out, mlp_gain, w_gate_ff, w_up, w_down)
    weights = tuple((member.astype(jnp.float32) for member in weights))
    output, pullback = jax.vjp(layer, inputs.astype(jnp.float32), *weights)
    grads = pullback(cotangent.astype(jnp.float32))
    return (output.astype(jnp.bfloat16), grads[0].astype(jnp.bfloat16), grads[1], grads[2], grads[3], grads[4], grads[5], grads[6], grads[7], grads[8], grads[9], grads[10], grads[11], grads[12], grads[13], grads[14])
```

```python
import functools

import jax
import jax.numpy as jnp
from jax import lax
from jax.experimental import pallas as pl
from jax.experimental.pallas import tpu as pltpu
from jax.sharding import PartitionSpec as P

HEADS = 4
KH = 128
VH = 256
BLOCK = 64


EPS = 1e-06
HIGH = lax.Precision.HIGHEST


MESH = pl.DeviceIdType.MESH
ROWS = 16
SMALL = 16


def ring_place(index, n):
    odd = index % 2
    return (1 - odd) * (index // 2) + odd * (n - 1 - index // 2)


def ring_index(place, n):
    place = (place + 2 * n) % n
    late = place // (n // 2)
    return (1 - late) * 2 * place + late * (2 * (n - 1 - place) + 1)


def greet(devices):
    barrier = pltpu.get_barrier_semaphore()
    for device in devices:
        pl.semaphore_signal(barrier, inc=1, device_id=device, device_id_type=MESH)
    pl.semaphore_wait(barrier, len(devices))


def halves(width):
    first = (width // 256) * 128
    return ((0, first), (first, width - first))


def gather_kernel(n, many, *refs):
    shards, wholes = refs[:many], refs[many : 2 * many]
    local_sem, ring_send, ring_recv, pair_send, pair_recv = refs[2 * many :]
    me, replica = lax.axis_index("seq"), lax.axis_index("dp")
    core = replica % 2
    place = ring_place(me, n)
    pair = (me, replica + 1 - 2 * core)
    onward = [(ring_index(place + 1, n), replica), (ring_index(place - 1, n), replica)]
    greet([*onward, pair])

    def piece(a, way, half):
        rows = shards[a].shape[0] // 2
        start, size = halves(shards[a].shape[1])[way]
        return (pl.ds(pl.multiple_of(half * rows, ROWS), rows), pl.ds(start, size))

    def block(way, k):
        return ring_index(place - k if way == 0 else place + k, n)

    def own(a):
        return pltpu.make_async_copy(shards[a], wholes[a].at[me], local_sem.at[a])

    def ring(way, k, a, arriving):
        where = piece(a, way, core)
        here = wholes[a].at[(block(way, k + 1 if arriving else k), *where)]
        return pltpu.make_async_remote_copy(
            src_ref=shards[a].at[where] if k == 0 and not arriving else here,
            dst_ref=here,
            send_sem=ring_send.at[way, k, a],
            recv_sem=ring_recv.at[way, k, a],
            device_id=onward[way],
            device_id_type=MESH,
        )

    def across(way, k, a, half):
        here = wholes[a].at[(block(way, k + 1), *piece(a, way, half))]
        return pltpu.make_async_remote_copy(
            src_ref=here,
            dst_ref=here,
            send_sem=pair_send.at[way, k, a],
            recv_sem=pair_recv.at[way, k, a],
            device_id=pair,
            device_id_type=MESH,
        )

    steps = [(k, a, way) for k in range(n - 1) for a in range(many) for way in range(2)]
    for k, a, way in steps:
        if k > 0:
            ring(way, k - 1, a, True).wait_recv()
        ring(way, k, a, False).start()
        if k > 0:
            across(way, k - 1, a, core).start()
    for a in range(many):
        own(a).start()
    for a in range(many):
        for way in range(2):
            ring(way, n - 2, a, True).wait_recv()
            across(way, n - 2, a, core).start()
    for k, a, way in steps:
        across(way, k, a, 1 - core).wait_recv()
    for k, a, way in steps:
        ring(way, k, a, False).wait_send()
        across(way, k, a, core).wait_send()
    for a in range(many):
        own(a).wait()


def gather_all(shards):
    n, many = lax.axis_size("seq"), len(shards)
    anywhere = pl.BlockSpec(memory_space=pl.ANY)
    sems = pltpu.SemaphoreType.DMA((2, n - 1, many))
    wholes = pl.pallas_call(
        functools.partial(gather_kernel, n, many),
        out_shape=[jax.ShapeDtypeStruct((n, *shard.shape), shard.dtype) for shard in shards],
        in_specs=[anywhere] * many,
        out_specs=[anywhere] * many,
        scratch_shapes=[pltpu.SemaphoreType.DMA((many,)), sems, sems, sems, sems],
        compiler_params=pltpu.CompilerParams(collective_id=0, has_side_effects=True),
    )(*shards)
    return [whole.reshape(-1, whole.shape[-1]) for whole in wholes]


def reduce_kernel(n, many, joined, *refs):
    grads, sums = refs[:many], refs[many : 2 * many]
    own, other, first, second, fresh = (refs[(2 + i) * many : (3 + i) * many] for i in range(5))
    (
        local_sem,
        pair_send,
        pair_recv,
        ring_send,
        ring_recv,
        peer_send,
        peer_recv,
        back_send,
        back_recv,
        out_sem,
    ) = refs[7 * many :]
    moving = (first, second)
    me, replica = lax.axis_index("seq"), lax.axis_index("dp")
    core = replica % 2
    place = ring_place(me, n)
    pair = (me, replica + 1 - 2 * core)
    peer = (me, (replica + 2) % 4)
    onward = [(ring_index(place + 1, n), replica), (ring_index(place - 1, n), replica)]
    greet([*onward, pair, peer] if joined else [*onward, pair])

    def rows_of(a, half):
        rows = grads[a].shape[1] // 2
        return pl.ds(pl.multiple_of(half * rows, ROWS), rows)

    def columns(a, way):
        start, size = halves(grads[a].shape[2])[way]
        return pl.ds(start, size)

    def block(way, k):
        return ring_index(place - 1 - k if way == 0 else place + 1 + k, n)

    def load(j, b, a):
        return pltpu.make_async_copy(
            grads[a].at[b, rows_of(a, core)], own[a].at[b], local_sem.at[j, a]
        )

    def across(j, b, a):
        return pltpu.make_async_remote_copy(
            src_ref=grads[a].at[b, rows_of(a, 1 - core)],
            dst_ref=other[a].at[b],
            send_sem=pair_send.at[j, a],
            recv_sem=pair_recv.at[j, a],
            device_id=pair,
            device_id_type=MESH,
        )

    def ring(way, k, a):
        source = own[a].at[block(way, 0), :, columns(a, way)] if k == 0 else moving[way][a].at[k - 1]
        return pltpu.make_async_remote_copy(
            src_ref=source,
            dst_ref=moving[way][a].at[k],
            send_sem=ring_send.at[way, k, a],
            recv_sem=ring_recv.at[way, k, a],
            device_id=onward[way],
            device_id_type=MESH,
        )

    def trade(way, a):
        return pltpu.make_async_remote_copy(
            src_ref=own[a].at[me, :, columns(a, way)],
            dst_ref=fresh[a].at[:, columns(a, way)],
            send_sem=peer_send.at[way, a],
            recv_sem=peer_recv.at[way, a],
            device_id=peer,
            device_id_type=MESH,
        )

    def put(a):
        return pltpu.make_async_copy(own[a].at[me], sums[a].at[rows_of(a, core)], out_sem.at[a])

    def back(a, half):
        return pltpu.make_async_remote_copy(
            src_ref=own[a].at[me],
            dst_ref=sums[a].at[rows_of(a, half)],
            send_sem=back_send.at[a],
            recv_sem=back_recv.at[a],
            device_id=pair,
            device_id_type=MESH,
        )

    def sweep(a, act):
        def turn(i, carry):
            act(pl.ds(pl.multiple_of(i * ROWS, ROWS), ROWS))
            return carry

        lax.fori_loop(0, grads[a].shape[1] // 2 // ROWS, turn, 0)

    order = []
    for k in range(n // 2):
        order.append(block(0, k))
        if len(order) < n - 1:
            order.append(block(1, k))
    order = order[: n - 1] + [me]
    for j, b in enumerate(order):
        for a in range(many):
            across(j, b, a).start()
            load(j, b, a).start()

    ready = set()

    def need(j, a):
        if (j, a) not in ready:
            ready.add((j, a))
            load(j, order[j], a).wait()
            across(j, order[j], a).wait_recv()

    def slot(way, k):
        if k == n - 1:
            return n - 1
        return 2 * k + way if 2 * k + way < n - 1 and k < n // 2 else 2 * (n - 2 - k) + 1 - way

    def add(way, k, a):
        need(slot(way, k), a)
        b, across_columns = block(way, k), columns(a, way)
        if k == 0 or k == n - 1:
            target, at = own[a], lambda rows: (b, rows, across_columns)
        else:
            target, at = moving[way][a], lambda rows: (k - 1, rows, slice(None))

        def act(rows):
            total = own[a][b, rows, across_columns].astype(jnp.float32)
            total = total + other[a][b, rows, across_columns].astype(jnp.float32)
            if k > 0:
                total = total + moving[way][a][k - 1, rows, :].astype(jnp.float32)
            target[at(rows)] = total.astype(jnp.bfloat16)

        sweep(a, act)

    for k in range(n):
        for a in range(many):
            for way in range(2):
                if k > 0:
                    ring(way, k - 1, a).wait_recv()
                add(way, k, a)
                if k < n - 1:
                    ring(way, k, a).start()
                elif joined:
                    trade(way, a).start()
    for a in range(many):
        if joined:
            for way in range(2):
                trade(way, a).wait()

            def act(rows):
                total = own[a][me, rows, :].astype(jnp.float32) + fresh[a][rows, :].astype(
                    jnp.float32
                )
                own[a][me, rows, :] = total.astype(jnp.bfloat16)

            sweep(a, act)
        put(a).start()
        back(a, core).start()
    for a in range(many):
        put(a).wait()
        back(a, core).wait_send()
        back(a, 1 - core).wait_recv()
    for k in range(n - 1):
        for a in range(many):
            for way in range(2):
                ring(way, k, a).wait_send()
    for j, b in enumerate(order):
        for a in range(many):
            across(j, b, a).wait_send()


def reduce_all(grads):
    n, many = lax.axis_size("seq"), len(grads)
    joined = lax.axis_size("dp") == 4
    blocks = [grad.reshape(n, -1, grad.shape[-1]) for grad in grads]
    anywhere = pl.BlockSpec(memory_space=pl.ANY)

    def buffers(count, way=None):
        shapes = []
        for part in blocks:
            width = part.shape[2] if way is None else halves(part.shape[2])[way][1]
            lead = () if count is None else (count,)
            shapes.append(pltpu.VMEM((*lead, part.shape[1] // 2, width), jnp.bfloat16))
        return shapes

    dma = pltpu.SemaphoreType.DMA
    sums = pl.pallas_call(
        functools.partial(reduce_kernel, n, many, joined),
        out_shape=[jax.ShapeDtypeStruct(part.shape[1:], jnp.bfloat16) for part in blocks],
        in_specs=[anywhere] * many,
        out_specs=[anywhere] * many,
        scratch_shapes=[
            *buffers(n),
            *buffers(n),
            *buffers(n - 1, 0),
            *buffers(n - 1, 1),
            *buffers(None),
            dma((n, many)),
            dma((n, many)),
            dma((n, many)),
            dma((2, n - 1, many)),
            dma((2, n - 1, many)),
            dma((2, many)),
            dma((2, many)),
            dma((many,)),
            dma((many,)),
            dma((many,)),
        ],
        compiler_params=pltpu.CompilerParams(
            collective_id=3, has_side_effects=True, vmem_limit_bytes=48 * 2**20
        ),
    )(*blocks)
    if joined:
        return sums
    core = lax.axis_index("dp") % 2
    total = []
    for part in sums:
        rows = lax.broadcasted_iota(jnp.int32, part.shape, 0)
        mine = rows // (part.shape[0] // 2) == core
        total.append(lax.psum(jnp.where(mine, part, 0).astype(jnp.bfloat16), "dp"))
    return total


def scan_kernel(n, reverse, x_ref, y_ref, held, sent, send_sem, recv_sem, out_send, out_recv):
    me, replica = lax.axis_index("seq"), lax.axis_index("dp")
    share = x_ref.shape[0] // n
    width = y_ref.shape[1]
    greet([((me + off) % n, replica) for off in range(1, n)])

    def span(index):
        return pl.ds(index * share, share)

    def spread(off):
        target = (me + off) % n
        return pltpu.make_async_remote_copy(
            src_ref=x_ref.at[span(target)],
            dst_ref=held.at[me],
            send_sem=send_sem.at[off - 1],
            recv_sem=recv_sem.at[off - 1],
            device_id=(target, replica),
            device_id_type=MESH,
        )

    def arrive(off):
        source = (me + n - off) % n
        return pltpu.make_async_remote_copy(
            src_ref=x_ref.at[span(me)],
            dst_ref=held.at[source],
            send_sem=send_sem.at[off - 1],
            recv_sem=recv_sem.at[off - 1],
            device_id=(source, replica),
            device_id_type=MESH,
        )

    def give(off):
        target = (me + off) % n
        return pltpu.make_async_remote_copy(
            src_ref=sent.at[target],
            dst_ref=y_ref.at[span(me)],
            send_sem=out_send.at[off - 1],
            recv_sem=out_recv.at[off - 1],
            device_id=(target, replica),
            device_id_type=MESH,
        )

    def take(off):
        source = (me + n - off) % n
        return pltpu.make_async_remote_copy(
            src_ref=sent.at[me],
            dst_ref=y_ref.at[span(source)],
            send_sem=out_send.at[off - 1],
            recv_sem=out_recv.at[off - 1],
            device_id=(source, replica),
            device_id_type=MESH,
        )

    for off in range(1, n):
        spread(off).start()
    held[me] = x_ref[span(me)]
    for off in range(1, n):
        arrive(off).wait_recv()
    for p in range(share):
        state = jnp.zeros(y_ref.shape[1:], jnp.float32)
        for s in range(n - 1, -1, -1) if reverse else range(n):
            sent[s, p] = state.astype(sent.dtype)
            passing = held[s, p, width : width + ROWS].astype(jnp.float32)[:1]
            state = passing * state + held[s, p, :width].astype(jnp.float32)
    for off in range(1, n):
        give(off).start()
    y_ref[span(me)] = sent[me]
    for off in range(1, n):
        take(off).wait_recv()
    for off in range(1, n):
        spread(off).wait_send()
        give(off).wait_send()


def entering(passing, deposit, reverse):
    n = lax.axis_size("seq")
    seqs, heads, values, keys = deposit.shape
    pairs = seqs * heads
    share = pairs // n
    tail = jnp.broadcast_to(passing.reshape(pairs, 1, keys), (pairs, ROWS, keys))
    packed = jnp.concatenate([deposit.reshape(pairs, values, keys), tail], axis=1)
    dma = pltpu.SemaphoreType.DMA((n - 1,))
    arrived = pl.pallas_call(
        functools.partial(scan_kernel, n, reverse),
        out_shape=jax.ShapeDtypeStruct((pairs, values, keys), jnp.bfloat16),
        in_specs=[pl.BlockSpec(memory_space=pltpu.VMEM)],
        out_specs=pl.BlockSpec(memory_space=pltpu.VMEM),
        scratch_shapes=[
            pltpu.VMEM((n, share, values + ROWS, keys), jnp.bfloat16),
            pltpu.VMEM((n, share, values, keys), jnp.bfloat16),
            dma,
            dma,
            dma,
            dma,
        ],
        compiler_params=pltpu.CompilerParams(
            collective_id=2 if reverse else 1,
            has_side_effects=True,
            vmem_limit_bytes=16 * 2**20,
        ),
    )(packed.astype(jnp.bfloat16))
    return arrived.reshape(seqs, heads, values, keys).swapaxes(2, 3).astype(jnp.float32)


def matmul(left, right):
    return jnp.dot(left, right, preferred_element_type=jnp.float32)


def inner_rows(left, right):
    return lax.dot_general(
        left, right, (((0,), (0,)), ((), ())), preferred_element_type=jnp.float32
    )


def times_transposed(left, right):
    return lax.dot_general(
        left, right, (((1,), (1,)), ((), ())), preferred_element_type=jnp.float32
    )


def rms_scale(source):
    return lax.rsqrt(jnp.mean(source * source, axis=-1, keepdims=True) + EPS)


def head_scale(source):
    return lax.rsqrt(jnp.maximum(jnp.mean(source * source, axis=-1, keepdims=True), 1.0))


def norm_back(grad_unit, unit, scale):
    return scale * (grad_unit - unit * jnp.mean(grad_unit * unit, axis=-1, keepdims=True))


def head_norm_back(grad_unit, unit, scale):
    live = jnp.where(scale < 1.0, 1.0, 0.0)
    return scale * (grad_unit - live * unit * jnp.mean(grad_unit * unit, axis=-1, keepdims=True))


def block_step(memory, pieces):
    queries, key_rows, values, log_decay = pieces
    running = jnp.cumsum(log_decay, axis=2)
    length = running.shape[2]
    target = lax.broadcasted_iota(jnp.int32, (length, length), 0)
    source = lax.broadcasted_iota(jnp.int32, (length, length), 1)
    causal = jnp.where(target >= source, 1.0, 0.0).astype(jnp.float32)
    rising = queries * jnp.exp(running)
    falling = key_rows * jnp.exp(-running)
    scores = jnp.einsum("bhtk,bhsk->bhts", rising, falling, precision=HIGH) * causal
    within = jnp.einsum("bhts,bhsv->bhtv", scores, values, precision=HIGH)
    across = jnp.einsum("bhtk,bhkv->bhtv", rising, memory, precision=HIGH)
    ending = running[:, :, -1:, :]
    carried = jnp.exp(ending - running) * key_rows
    deposit = jnp.einsum("bhsk,bhsv->bhkv", carried, values, precision=HIGH)
    return (jnp.exp(ending[:, :, 0, :])[:, :, :, None] * memory + deposit, within + across)


def to_blocks(source, width):
    seqs, span = (source.shape[0], source.shape[1])
    blocked = source.reshape(seqs, span // BLOCK, BLOCK, HEADS, width)
    return blocked.transpose(1, 0, 3, 2, 4)


def span_attention(queries, key_rows, values, log_decay, memory_in):
    seqs, span = (queries.shape[0], queries.shape[1])
    pieces = (
        to_blocks(queries, KH),
        to_blocks(key_rows, KH),
        to_blocks(values, VH),
        to_blocks(log_decay, KH),
    )
    memory_out, blocks_out = lax.scan(jax.checkpoint(block_step), memory_in, pieces)
    return (blocks_out.transpose(1, 0, 3, 2, 4).reshape(seqs, span, HEADS * VH), memory_out)


def forward(whole, inputs):
    (
        attn_gain,
        w_query,
        w_key,
        w_value,
        w_gate,
        w_rank_in,
        w_rank_out,
        rank_bias,
        out_gain,
        w_out,
        mlp_gain,
        w_gate_ff,
        w_up,
        w_down,
    ) = whole
    seqs, span, width = inputs.shape
    count = seqs * span
    rows_in = inputs.astype(jnp.float32).reshape(count, width)
    scale_in = rms_scale(rows_in)
    unit_in = rows_in * scale_in
    normed_in = (unit_in * attn_gain.astype(jnp.float32)).astype(jnp.bfloat16)
    queries = matmul(normed_in, w_query).astype(jnp.bfloat16)
    key_rows = matmul(normed_in, w_key).astype(jnp.bfloat16)
    values = matmul(normed_in, w_value).astype(jnp.bfloat16)
    gate_out = matmul(normed_in, w_gate)
    rank_rows = matmul(normed_in, w_rank_in)
    logits = jnp.dot(rank_rows, w_rank_out.astype(jnp.float32), precision=HIGH) + rank_bias.astype(
        jnp.float32
    )
    log_decay = (jax.nn.log_sigmoid(logits) / 16.0).reshape(seqs, span, HEADS * KH)
    scaled_queries = (queries.astype(jnp.float32) * KH ** (-0.5)).reshape(seqs, span, HEADS * KH)
    key_float = key_rows.astype(jnp.float32).reshape(seqs, span, HEADS * KH)
    value_float = values.astype(jnp.float32).reshape(seqs, span, HEADS * VH)
    running = jnp.cumsum(log_decay.reshape(seqs, span, HEADS, KH), axis=1)
    ending = running[:, -1]
    weighted_keys = jnp.exp(ending[:, None] - running) * key_float.reshape(seqs, span, HEADS, KH)
    deposit = jnp.einsum(
        "snhk,snhv->shvk", weighted_keys, value_float.reshape(seqs, span, HEADS, VH), precision=HIGH
    )
    passing = jnp.exp(ending)
    memory_in = entering(passing, deposit, False)
    mixed, memory_out = span_attention(scaled_queries, key_float, value_float, log_decay, memory_in)
    mixed_heads = mixed.reshape(count, HEADS, VH)
    scale_heads = head_scale(mixed_heads)
    unit_heads = mixed_heads * scale_heads
    heads_normed = (unit_heads * out_gain.astype(jnp.float32)).reshape(count, HEADS * VH)
    gated = (heads_normed * jax.nn.silu(gate_out)).astype(jnp.bfloat16)
    middle = rows_in + matmul(gated, w_out)
    scale_mid = rms_scale(middle)
    unit_mid = middle * scale_mid
    normed_mid = (unit_mid * mlp_gain.astype(jnp.float32)).astype(jnp.bfloat16)
    gate_ff = matmul(normed_mid, w_gate_ff)
    up_rows = matmul(normed_mid, w_up)
    hidden = (jax.nn.silu(gate_ff) * up_rows).astype(jnp.bfloat16)
    output = (middle + matmul(hidden, w_down)).astype(jnp.bfloat16).reshape(seqs, span, width)
    return (
        unit_in,
        scale_in,
        normed_in,
        scaled_queries,
        key_float,
        value_float,
        log_decay,
        running,
        memory_in,
        gate_out,
        rank_rows,
        logits,
        unit_heads,
        scale_heads,
        gated,
        unit_mid,
        scale_mid,
        normed_mid,
        gate_ff,
        up_rows,
        hidden,
        output,
    )


def backward(whole, kept, cotangent):
    (
        attn_gain,
        w_query,
        w_key,
        w_value,
        w_gate,
        w_rank_in,
        w_rank_out,
        rank_bias,
        out_gain,
        w_out,
        mlp_gain,
        w_gate_ff,
        w_up,
        w_down,
    ) = whole
    (
        unit_in,
        scale_in,
        normed_in,
        scaled_queries,
        key_float,
        value_float,
        log_decay,
        running,
        memory_in,
        gate_out,
        rank_rows,
        logits,
        unit_heads,
        scale_heads,
        gated,
        unit_mid,
        scale_mid,
        normed_mid,
        gate_ff,
        up_rows,
        hidden,
        output,
    ) = kept
    seqs, span, width = cotangent.shape
    count = seqs * span
    grad_rows = cotangent.reshape(count, width)
    grad_down = inner_rows(hidden, grad_rows)
    grad_hidden = times_transposed(grad_rows, w_down)
    sig_ff = jax.nn.sigmoid(gate_ff)
    slope_ff = sig_ff * (1.0 + gate_ff * (1.0 - sig_ff))
    grad_gate_ff = (grad_hidden * up_rows * slope_ff).astype(jnp.bfloat16)
    grad_up_rows = (grad_hidden * gate_ff * sig_ff).astype(jnp.bfloat16)
    grad_gate_ff_w = inner_rows(normed_mid, grad_gate_ff)
    grad_up_w = inner_rows(normed_mid, grad_up_rows)
    grad_normed_mid = times_transposed(grad_gate_ff, w_gate_ff) + times_transposed(
        grad_up_rows, w_up
    )
    grad_mlp_gain = jnp.sum(grad_normed_mid * unit_mid, axis=0)
    grad_middle = grad_rows.astype(jnp.float32) + norm_back(
        grad_normed_mid * mlp_gain.astype(jnp.float32), unit_mid, scale_mid
    )
    grad_branch = grad_middle.astype(jnp.bfloat16)
    grad_out_w = inner_rows(gated, grad_branch)
    grad_gated = times_transposed(grad_branch, w_out)
    sig_out = jax.nn.sigmoid(gate_out)
    slope_out = sig_out * (1.0 + gate_out * (1.0 - sig_out))
    gain_float = out_gain.astype(jnp.float32)
    heads_normed = (unit_heads * gain_float).reshape(count, HEADS * VH)
    grad_gate_out = (grad_gated * heads_normed * slope_out).astype(jnp.bfloat16)
    grad_heads = (grad_gated * gate_out * sig_out).reshape(count, HEADS, VH)
    grad_out_gain = jnp.sum(grad_heads * unit_heads, axis=(0, 1))
    grad_mixed = head_norm_back(grad_heads * gain_float, unit_heads, scale_heads).reshape(
        seqs, span, HEADS * VH
    )
    growth = jnp.exp(running)
    local_pull = jnp.einsum(
        "snhk,snhv->shvk",
        scaled_queries.reshape(seqs, span, HEADS, KH) * growth,
        grad_mixed.reshape(seqs, span, HEADS, VH),
        precision=HIGH,
    )
    passing = jnp.exp(running[:, -1])
    returned = entering(passing, local_pull, True)

    def local_span(first, second, third, fourth):
        return span_attention(first, second, third, fourth, memory_in)

    unused, pullback = jax.vjp(local_span, scaled_queries, key_float, value_float, log_decay)
    grad_scaled, grad_key_float, grad_value_float, grad_decay = pullback((grad_mixed, returned))
    grad_queries = (grad_scaled.reshape(count, HEADS * KH) * KH ** (-0.5)).astype(jnp.bfloat16)
    grad_keys = grad_key_float.reshape(count, HEADS * KH).astype(jnp.bfloat16)
    grad_values = grad_value_float.reshape(count, HEADS * VH).astype(jnp.bfloat16)
    grad_logits = grad_decay.reshape(count, HEADS * KH) * jax.nn.sigmoid(-logits) / 16.0
    grad_bias = jnp.sum(grad_logits, axis=0)
    grad_rank_out = jnp.einsum("rq,rk->qk", rank_rows, grad_logits, precision=HIGH)
    grad_rank_rows = jnp.einsum(
        "rk,qk->rq", grad_logits, w_rank_out.astype(jnp.float32), precision=HIGH
    )
    grad_rank_in = jnp.einsum(
        "rd,rq->dq", normed_in.astype(jnp.float32), grad_rank_rows, precision=HIGH
    )
    grad_query_w = inner_rows(normed_in, grad_queries)
    grad_key_w = inner_rows(normed_in, grad_keys)
    grad_value_w = inner_rows(normed_in, grad_values)
    grad_gate_w = inner_rows(normed_in, grad_gate_out)
    grad_normed_in = times_transposed(grad_queries, w_query) + times_transposed(grad_keys, w_key)
    grad_normed_in = (
        grad_normed_in
        + times_transposed(grad_values, w_value)
        + times_transposed(grad_gate_out, w_gate)
    )
    grad_normed_in = grad_normed_in + jnp.einsum(
        "rq,dq->rd", grad_rank_rows, w_rank_in.astype(jnp.float32), precision=HIGH
    )
    grad_attn_gain = jnp.sum(grad_normed_in * unit_in, axis=0)
    input_grad = grad_middle + norm_back(
        grad_normed_in * attn_gain.astype(jnp.float32), unit_in, scale_in
    )
    grads = (
        grad_attn_gain,
        grad_query_w,
        grad_key_w,
        grad_value_w,
        grad_gate_w,
        grad_rank_in,
        grad_rank_out,
        grad_bias,
        grad_out_gain,
        grad_out_w,
        grad_mlp_gain,
        grad_gate_ff_w,
        grad_up_w,
        grad_down,
    )
    return (grads, input_grad.astype(jnp.bfloat16).reshape(seqs, span, width))


def body(
    inputs,
    cotangent,
    attn_gain,
    w_query,
    w_key,
    w_value,
    w_gate,
    w_rank_in,
    w_rank_out,
    rank_bias,
    out_gain,
    w_out,
    mlp_gain,
    w_gate_ff,
    w_up,
    w_down,
):
    n = lax.axis_size("seq")
    gains = (attn_gain, w_rank_out, rank_bias, out_gain, mlp_gain)
    rows = w_query.shape[0]
    flat = jnp.concatenate([gain.reshape(-1) for gain in gains])
    flat = jnp.pad(flat, (0, rows * SMALL - flat.size)).reshape(rows, SMALL)
    spare = jnp.zeros((rows, 128 - w_rank_in.shape[1] - SMALL), w_query.dtype)
    mixer = jnp.concatenate([w_query, w_key, w_value, w_gate, w_out, w_rank_in, flat, spare], axis=1)
    up_pair = jnp.concatenate([w_gate_ff, w_up], axis=1)
    mixer, up_pair, down = gather_all([mixer, up_pair, w_down])
    cuts = [0]
    for weight in (w_query, w_key, w_value, w_gate, w_out, w_rank_in):
        cuts.append(cuts[-1] + weight.shape[1])
    parts = [mixer[:, low:high] for low, high in zip(cuts[:-1], cuts[1:])]
    flat = mixer[:, cuts[-1] : cuts[-1] + SMALL].reshape(n, rows * SMALL)
    small, at = [], 0
    for gain in gains:
        piece = flat[:, at : at + gain.size].reshape(n * gain.shape[0], *gain.shape[1:])
        small.append(piece)
        at += gain.size
    whole = (
        small[0],
        parts[0],
        parts[1],
        parts[2],
        parts[3],
        parts[5],
        small[1],
        small[2],
        small[3],
        parts[4],
        small[4],
        up_pair[:, : w_gate_ff.shape[1]],
        up_pair[:, w_gate_ff.shape[1] :],
        down,
    )
    kept = forward(whole, inputs)
    output = kept[-1]
    grads, input_grad = backward(whole, kept, cotangent)
    low = [grad.astype(jnp.bfloat16) for grad in grads]
    flat = jnp.concatenate(
        [low[i].reshape(n, -1) for i in (0, 6, 7, 8, 10)], axis=1
    )
    flat = jnp.pad(flat, ((0, 0), (0, rows * SMALL - flat.shape[1]))).reshape(n * rows, SMALL)
    spare = jnp.zeros((n * rows, spare.shape[1]), jnp.bfloat16)
    mixer = jnp.concatenate(
        [low[1], low[2], low[3], low[4], low[9], low[5], flat, spare], axis=1
    )
    mixer, up_pair, down = reduce_all([mixer, jnp.concatenate([low[11], low[12]], axis=1), low[13]])
    mixer, up_pair = mixer.astype(jnp.float32), up_pair.astype(jnp.float32)
    parts = [mixer[:, start:end] for start, end in zip(cuts[:-1], cuts[1:])]
    flat = mixer[:, cuts[-1] : cuts[-1] + SMALL].reshape(-1)
    small, at = [], 0
    for gain in gains:
        small.append(flat[at : at + gain.size].reshape(gain.shape))
        at += gain.size
    summed = (
        small[0],
        parts[0],
        parts[1],
        parts[2],
        parts[3],
        parts[5],
        small[1],
        small[2],
        small[3],
        parts[4],
        small[4],
        up_pair[:, : w_gate_ff.shape[1]],
        up_pair[:, w_gate_ff.shape[1] :],
        down.astype(jnp.float32),
    )
    return (
        output,
        input_grad,
        summed[0],
        summed[1],
        summed[2],
        summed[3],
        summed[4],
        summed[5],
        summed[6],
        summed[7],
        summed[8],
        summed[9],
        summed[10],
        summed[11],
        summed[12],
        summed[13],
    )


def solution(mesh):
    placed = (
        P("dp", "seq", None),
        P("dp", "seq", None),
        P("seq"),
        P("seq", None),
        P("seq", None),
        P("seq", None),
        P("seq", None),
        P("seq", None),
        P("seq", None),
        P("seq"),
        P("seq"),
        P("seq", None),
        P("seq"),
        P("seq", None),
        P("seq", None),
        P("seq", None),
    )
    return jax.shard_map(
        body,
        mesh=mesh,
        in_specs=placed,
        out_specs=(
            P("dp", "seq", None),
            P("dp", "seq", None),
            P("seq"),
            P("seq", None),
            P("seq", None),
            P("seq", None),
            P("seq", None),
            P("seq", None),
            P("seq", None),
            P("seq"),
            P("seq"),
            P("seq", None),
            P("seq"),
            P("seq", None),
            P("seq", None),
            P("seq", None),
        ),
        check_vma=False,
    )
```

```python
import functools

import jax
import jax.numpy as jnp
from jax import lax
from jax.experimental import pallas as pl
from jax.experimental.pallas import tpu as pltpu
from jax.sharding import PartitionSpec as P

HEADS = 4
KH = 128
VH = 256
BLOCK = 64


EPS = 1e-06
HIGH = lax.Precision.HIGHEST


MESH = pl.DeviceIdType.MESH
ROWS = 16
SMALL = 16
IN_VMEM = pl.BlockSpec(memory_space=pltpu.VMEM)


def ring_place(index, n):
    odd = index % 2
    return (1 - odd) * (index // 2) + odd * (n - 1 - index // 2)


def ring_index(place, n):
    place = (place + 2 * n) % n
    late = place // (n // 2)
    return (1 - late) * 2 * place + late * (2 * (n - 1 - place) + 1)


def greet(devices):
    barrier = pltpu.get_barrier_semaphore()
    for device in devices:
        pl.semaphore_signal(barrier, inc=1, device_id=device, device_id_type=MESH)
    pl.semaphore_wait(barrier, len(devices))


def split_columns(width):
    side = (width // 128 + 1) // 3 * 128
    return (side, width - 2 * side)


def partners(n):
    me, replica = lax.axis_index("seq"), lax.axis_index("dp")
    core, plane = replica % 2, (replica // 2) % 2
    place = ring_place(me, n)
    pair = (me, replica + 1 - 2 * core)
    peer = (me, replica + 2 - 4 * plane)
    onward = [(ring_index(place + 1, n), replica), (ring_index(place - 1, n), replica)]
    return (me, core, plane, place, pair, peer, onward)


def class_columns(width, way, plane):
    side, rest = split_columns(width)
    if way == 0:
        return pl.ds(pl.multiple_of(plane * side, 128), side)
    return pl.ds(2 * side, rest)


def cut(refs, sizes):
    pieces, at = [], 0
    for size in sizes:
        pieces.append(refs[at : at + size])
        at += size
    return (*pieces, refs[at:])


def everyone(n):
    me, replica = lax.axis_index("seq"), lax.axis_index("dp")
    return [((me + off) % n, replica) for off in range(1, n)]


def gather_kernel(n, many, layout, beside, given, made, *refs):
    shards, beside_in, wholes, beside_out, held, sems, beside_scratch = cut(
        refs, (len(layout), given, many, made, many, 9)
    )
    count = len(layout)
    work = beside(n, *beside_in, *beside_out, *beside_scratch) if beside else None
    (
        load_sem,
        own_sem,
        ring_send,
        ring_recv,
        peer_send,
        peer_recv,
        pair_send,
        pair_recv,
        out_sem,
    ) = sems
    me, core, plane, place, pair, peer, onward = partners(n)

    def load(i):
        a, start, width = layout[i]
        return pltpu.make_async_copy(
            shards[i], held[a].at[me, :, pl.ds(start, width)], load_sem.at[i]
        )

    for i in range(count):
        load(i).start()
    greet([*(everyone(n) if beside else onward), pair, peer])

    def half_rows(a, half):
        rows = held[a].shape[1] // 2
        return pl.ds(pl.multiple_of(half * rows, ROWS), rows)

    def block(way, k):
        return ring_index(place - k if way == 0 else place + k, n)

    def own(a):
        return pltpu.make_async_copy(held[a].at[me], wholes[a].at[me], own_sem.at[a])

    def remote(here, send, recv, device):
        return pltpu.make_async_remote_copy(
            src_ref=here,
            dst_ref=here,
            send_sem=send,
            recv_sem=recv,
            device_id=device,
            device_id_type=MESH,
        )

    def ring(way, k, a, arriving):
        columns = class_columns(held[a].shape[2], way, plane)
        here = held[a].at[block(way, k + 1 if arriving else k), half_rows(a, core), columns]
        return remote(here, ring_send.at[way, k, a], ring_recv.at[way, k, a], onward[way])

    def swap(k, a, side):
        columns = class_columns(held[a].shape[2], 0, side)
        here = held[a].at[block(0, k + 1), half_rows(a, core), columns]
        return remote(here, peer_send.at[k, a], peer_recv.at[k, a], peer)

    def group(a, way):
        side, rest = split_columns(held[a].shape[2])
        return pl.ds(0, 2 * side) if way == 0 else pl.ds(2 * side, rest)

    def across(way, k, a, half):
        here = held[a].at[block(way, k + 1), half_rows(a, half), group(a, way)]
        return remote(here, pair_send.at[way, k, a], pair_recv.at[way, k, a], pair)

    def put(way, k, a):
        where = (block(way, k + 1), slice(None), group(a, way))
        return pltpu.make_async_copy(
            held[a].at[where], wholes[a].at[where], out_sem.at[way, k, a]
        )

    for i in range(count):
        load(i).wait()
    for k in range(n + 2):
        for a in range(many):
            for way in range(2):
                if 0 <= k - 1 < n - 1:
                    ring(way, k - 1, a, True).wait_recv()
                if k < n - 1:
                    ring(way, k, a, False).start()
                if 0 <= k - 1 < n - 1:
                    if way == 0:
                        swap(k - 1, a, plane).start()
                    else:
                        across(1, k - 1, a, core).start()
        if k == 0:
            for a in range(many):
                own(a).start()
        for a in range(many):
            if 0 <= k - 2 < n - 1:
                swap(k - 2, a, 1 - plane).wait_recv()
                across(0, k - 2, a, core).start()
        for a in range(many):
            for way in range(2):
                if 0 <= k - 3 < n - 1:
                    across(way, k - 3, a, 1 - core).wait_recv()
                    put(way, k - 3, a).start()
        if work:
            work(k)
    for k in range(n - 1):
        for a in range(many):
            swap(k, a, plane).wait_send()
            for way in range(2):
                ring(way, k, a, False).wait_send()
                across(way, k, a, core).wait_send()
                put(way, k, a).wait()
    for a in range(many):
        own(a).wait()


def gather_all(groups, collective_id, beside=None, operands=(), results=(), scratch=()):
    n, many = lax.axis_size("seq"), len(groups)
    anywhere = pl.BlockSpec(memory_space=pl.ANY)
    dma = pltpu.SemaphoreType.DMA
    layout, shards, shapes = [], [], []
    for a, group in enumerate(groups):
        start = 0
        for shard in group:
            layout.append((a, start, shard.shape[1]))
            shards.append(shard)
            start += shard.shape[1]
        shapes.append((n, group[0].shape[0], start))
    ring, single = dma((2, n - 1, many)), dma((n - 1, many))
    wholes = pl.pallas_call(
        functools.partial(
            gather_kernel, n, many, tuple(layout), beside, len(operands), len(results)
        ),
        out_shape=[*[jax.ShapeDtypeStruct(shape, jnp.bfloat16) for shape in shapes], *results],
        in_specs=[anywhere] * len(shards) + [IN_VMEM] * len(operands),
        out_specs=[anywhere] * many + [IN_VMEM] * len(results),
        scratch_shapes=[
            *[pltpu.VMEM(shape, jnp.bfloat16) for shape in shapes],
            dma((len(shards),)),
            dma((many,)),
            ring,
            ring,
            single,
            single,
            ring,
            ring,
            ring,
            *scratch,
        ],
        compiler_params=pltpu.CompilerParams(
            collective_id=collective_id, has_side_effects=True, vmem_limit_bytes=48 * 2**20
        ),
    )(*shards, *operands)
    return [*[whole.reshape(-1, whole.shape[-1]) for whole in wholes[:many]], *wholes[many:]]


def reduce_kernel(n, many, joined, beside, given, made, *refs):
    grads, beside_in, sums, beside_out, buffers, sems, beside_scratch = cut(
        refs, (many, given, many, made, 7 * many, 12)
    )
    work = beside(n, *beside_in, *beside_out, *beside_scratch) if beside else None
    own, other, first, second, swapped, fresh, landed, _ = cut(buffers, (many,) * 7)
    (
        local_sem,
        pair_send,
        pair_recv,
        ring_send,
        ring_recv,
        swap_send,
        swap_recv,
        peer_send,
        peer_recv,
        back_send,
        back_recv,
        out_sem,
    ) = sems
    moving = (first, second)
    me, core, plane, place, pair, peer, onward = partners(n)
    greet([*(everyone(n) if beside else onward), pair, peer])

    def rows_of(a, half):
        rows = grads[a].shape[1] // 2
        return pl.ds(pl.multiple_of(half * rows, ROWS), rows)

    def columns(a, way, side=None):
        return class_columns(grads[a].shape[2], way, plane if side is None else side)

    def block(way, k):
        return ring_index(place - 1 - k if way == 0 else place + 1 + k, n)

    def remote(source, target, send, recv, device):
        return pltpu.make_async_remote_copy(
            src_ref=source,
            dst_ref=target,
            send_sem=send,
            recv_sem=recv,
            device_id=device,
            device_id_type=MESH,
        )

    def load(j, b, a):
        return pltpu.make_async_copy(
            grads[a].at[b, rows_of(a, core)], own[a].at[b], local_sem.at[j, a]
        )

    def across(j, b, a):
        return remote(
            grads[a].at[b, rows_of(a, 1 - core)],
            other[a].at[b],
            pair_send.at[j, a],
            pair_recv.at[j, a],
            pair,
        )

    def ring(way, k, a):
        source = own[a].at[block(way, 0), :, columns(a, way)] if k == 0 else moving[way][a].at[k - 1]
        return remote(
            source,
            moving[way][a].at[k],
            ring_send.at[way, k, a],
            ring_recv.at[way, k, a],
            onward[way],
        )

    def swap(k, a):
        return remote(
            own[a].at[block(0, k), :, columns(a, 0, 1 - plane)],
            swapped[a].at[k],
            swap_send.at[k, a],
            swap_recv.at[k, a],
            peer,
        )

    def trade(a):
        return remote(
            own[a].at[me, :, columns(a, 1)],
            fresh[a],
            peer_send.at[1, a],
            peer_recv.at[1, a],
            peer,
        )

    def finish(a):
        here = own[a].at[me, :, columns(a, 0)]
        return remote(here, landed[a], peer_send.at[0, a], peer_recv.at[0, a], peer)

    def put(a):
        return pltpu.make_async_copy(own[a].at[me], sums[a].at[rows_of(a, core)], out_sem.at[a])

    def back(a, half):
        return remote(
            own[a].at[me], sums[a].at[rows_of(a, half)], back_send.at[a], back_recv.at[a], pair
        )

    def sweep(a, act):
        def turn(i, carry):
            act(pl.ds(pl.multiple_of(i * ROWS, ROWS), ROWS))
            return carry

        lax.fori_loop(0, grads[a].shape[1] // 2 // ROWS, turn, 0)

    order = []
    for k in range(n // 2):
        order.append(block(0, k))
        if len(order) < n - 1:
            order.append(block(1, k))
    order = order[: n - 1] + [me]
    for j, b in enumerate(order):
        for a in range(many):
            across(j, b, a).start()
            load(j, b, a).start()

    ready = set()

    def need(j, a):
        if (j, a) not in ready:
            ready.add((j, a))
            load(j, order[j], a).wait()
            across(j, order[j], a).wait_recv()

    def slot(way, k):
        if k == n - 1:
            return n - 1
        return 2 * k + way if 2 * k + way < n - 1 and k < n // 2 else 2 * (n - 2 - k) + 1 - way

    def hand_over(k, a):
        need(slot(0, k), a)
        b, theirs = block(0, k), columns(a, 0, 1 - plane)

        def act(rows):
            total = own[a][b, rows, theirs].astype(jnp.float32)
            total = total + other[a][b, rows, theirs].astype(jnp.float32)
            own[a][b, rows, theirs] = total.astype(jnp.bfloat16)

        sweep(a, act)
        swap(k, a).start()

    def add(way, k, a):
        need(slot(way, k), a)
        b, mine = block(way, k), columns(a, way)
        if way == 0:
            swap(k, a).wait_recv()
        if k > 0:
            ring(way, k - 1, a).wait_recv()

        def act(rows):
            total = own[a][b, rows, mine].astype(jnp.float32)
            total = total + other[a][b, rows, mine].astype(jnp.float32)
            if way == 0:
                total = total + swapped[a][k, rows, :].astype(jnp.float32)
            if k > 0:
                total = total + moving[way][a][k - 1, rows, :].astype(jnp.float32)
            if k == 0 or k == n - 1:
                own[a][b, rows, mine] = total.astype(jnp.bfloat16)
            else:
                moving[way][a][k - 1, rows, :] = total.astype(jnp.bfloat16)

        sweep(a, act)

    for k in range(n):
        for a in range(many):
            if k == 0:
                hand_over(0, a)
        for a in range(many):
            for way in (1, 0):
                add(way, k, a)
                if k < n - 1:
                    ring(way, k, a).start()
            if k < n - 1:
                hand_over(k + 1, a)
            elif joined:
                swap(k, a).wait_send()
                finish(a).start()
                trade(a).start()
        if work:
            work(k)
    for a in range(many):
        if joined:
            trade(a).wait()
            finish(a).wait()
            shared, theirs = columns(a, 1), columns(a, 0, 1 - plane)

            def act(rows):
                total = own[a][me, rows, shared].astype(jnp.float32)
                total = total + fresh[a][rows, :].astype(jnp.float32)
                own[a][me, rows, shared] = total.astype(jnp.bfloat16)
                own[a][me, rows, theirs] = landed[a][rows, :]

            sweep(a, act)
        else:
            swap(n - 1, a).wait_send()
        put(a).start()
        back(a, core).start()
    for a in range(many):
        put(a).wait()
        back(a, core).wait_send()
        back(a, 1 - core).wait_recv()
    for k in range(n - 1):
        for a in range(many):
            swap(k, a).wait_send()
            for way in range(2):
                ring(way, k, a).wait_send()
    for j, b in enumerate(order):
        for a in range(many):
            across(j, b, a).wait_send()


def reduce_all(grads, collective_id, beside=None, operands=(), results=(), scratch=()):
    n, many = lax.axis_size("seq"), len(grads)
    joined = lax.axis_size("dp") == 4
    blocks = [grad.reshape(n, -1, grad.shape[-1]) for grad in grads]
    anywhere = pl.BlockSpec(memory_space=pl.ANY)

    def buffers(count, way=None):
        shapes = []
        for part in blocks:
            width = part.shape[2] if way is None else split_columns(part.shape[2])[way]
            lead = () if count is None else (count,)
            shapes.append(pltpu.VMEM((*lead, part.shape[1] // 2, width), jnp.bfloat16))
        return shapes

    dma = pltpu.SemaphoreType.DMA
    sums = pl.pallas_call(
        functools.partial(reduce_kernel, n, many, joined, beside, len(operands), len(results)),
        out_shape=[
            *[jax.ShapeDtypeStruct(part.shape[1:], jnp.bfloat16) for part in blocks],
            *results,
        ],
        in_specs=[anywhere] * many + [IN_VMEM] * len(operands),
        out_specs=[anywhere] * many + [IN_VMEM] * len(results),
        scratch_shapes=[
            *buffers(n),
            *buffers(n),
            *buffers(n - 1, 0),
            *buffers(n - 1, 1),
            *buffers(n, 0),
            *buffers(None, 1),
            *buffers(None, 0),
            dma((n, many)),
            dma((n, many)),
            dma((n, many)),
            dma((2, n - 1, many)),
            dma((2, n - 1, many)),
            dma((n, many)),
            dma((n, many)),
            dma((2, many)),
            dma((2, many)),
            dma((many,)),
            dma((many,)),
            dma((many,)),
            *scratch,
        ],
        compiler_params=pltpu.CompilerParams(
            collective_id=collective_id, has_side_effects=True, vmem_limit_bytes=52 * 2**20
        ),
    )(*blocks, *operands)
    if joined:
        return sums
    sums, made = sums[:many], sums[many:]
    replica = lax.axis_index("dp")
    core, plane = replica % 2, (replica // 2) % 2
    total = []
    for part in sums:
        side = split_columns(part.shape[1])[0]
        rows = lax.broadcasted_iota(jnp.int32, part.shape, 0)
        kind = lax.broadcasted_iota(jnp.int32, part.shape, 1) // side
        mine = (rows // (part.shape[0] // 2) == core) & ((kind >= 2) | (kind == plane))
        total.append(lax.psum(jnp.where(mine, part, 0).astype(jnp.bfloat16), "dp"))
    return [*total, *made]


def scan_steps(n, reverse, x_ref, y_ref, held, sent, send_sem, recv_sem, out_send, out_recv):
    me, replica = lax.axis_index("seq"), lax.axis_index("dp")
    share = x_ref.shape[0] // n
    width = y_ref.shape[1]

    def span(index):
        return pl.ds(index * share, share)

    def spread(off):
        target = (me + off) % n
        return pltpu.make_async_remote_copy(
            src_ref=x_ref.at[span(target)],
            dst_ref=held.at[me],
            send_sem=send_sem.at[off - 1],
            recv_sem=recv_sem.at[off - 1],
            device_id=(target, replica),
            device_id_type=MESH,
        )

    def arrive(off):
        source = (me + n - off) % n
        return pltpu.make_async_remote_copy(
            src_ref=x_ref.at[span(me)],
            dst_ref=held.at[source],
            send_sem=send_sem.at[off - 1],
            recv_sem=recv_sem.at[off - 1],
            device_id=(source, replica),
            device_id_type=MESH,
        )

    def give(off):
        target = (me + off) % n
        return pltpu.make_async_remote_copy(
            src_ref=sent.at[target],
            dst_ref=y_ref.at[span(me)],
            send_sem=out_send.at[off - 1],
            recv_sem=out_recv.at[off - 1],
            device_id=(target, replica),
            device_id_type=MESH,
        )

    def take(off):
        source = (me + n - off) % n
        return pltpu.make_async_remote_copy(
            src_ref=sent.at[me],
            dst_ref=y_ref.at[span(source)],
            send_sem=out_send.at[off - 1],
            recv_sem=out_recv.at[off - 1],
            device_id=(source, replica),
            device_id_type=MESH,
        )

    def begin():
        for off in range(1, n):
            spread(off).start()
        held[me] = x_ref[span(me)]

    def carry():
        for off in range(1, n):
            arrive(off).wait_recv()
        for p in range(share):
            state = jnp.zeros(y_ref.shape[1:], jnp.float32)
            for s in range(n - 1, -1, -1) if reverse else range(n):
                sent[s, p] = state.astype(sent.dtype)
                passing = held[s, p, width : width + ROWS].astype(jnp.float32)[:1]
                state = passing * state + held[s, p, :width].astype(jnp.float32)
        for off in range(1, n):
            give(off).start()
        y_ref[span(me)] = sent[me]

    def end():
        for off in range(1, n):
            take(off).wait_recv()
        for off in range(1, n):
            spread(off).wait_send()
            give(off).wait_send()

    return (begin, carry, end)


def scan_scratch(pairs, n):
    share = pairs // n
    return [
        pltpu.VMEM((pairs, VH + ROWS, KH), jnp.bfloat16),
        pltpu.VMEM((n, share, VH + ROWS, KH), jnp.bfloat16),
        pltpu.VMEM((n, share, VH, KH), jnp.bfloat16),
        *[pltpu.SemaphoreType.DMA((n - 1,))] * 4,
    ]


def each_head(pairs, span, act):
    def turn(p, carry):
        seq, head = p // HEADS, p % HEADS
        rows = pl.ds(pl.multiple_of(seq * span, span), span)

        def keys(ref):
            return ref.at[rows, pl.ds(pl.multiple_of(head * KH, KH), KH)]

        def values(ref):
            return ref.at[rows, pl.ds(pl.multiple_of(head * VH, VH), VH)]

        def state(ref):
            return ref.at[pl.ds(p, 1)]

        act(keys, values, state)
        return carry

    lax.fori_loop(0, pairs, turn, 0)


def forward_beside(
    n, q, k, v, logits, gate, gain, mixed, gated, running, memory, packed, held, sent, *sems
):
    pairs = packed.shape[0]
    span = q.shape[0] // (pairs // HEADS)
    begin, carry, end = scan_steps(n, False, packed, memory, held, sent, *sems)

    def deposit(keys, values, state):
        deposit_kernel(keys(k), values(v), keys(logits), keys(running), state(packed))

    def mix(keys, values, state):
        mix_kernel(
            keys(q),
            keys(k),
            values(v),
            keys(running),
            state(memory),
            values(gate),
            gain,
            values(mixed),
            values(gated),
        )

    def work(step):
        if step == 0:
            each_head(pairs, span, deposit)
            begin()
        if step == 3:
            carry()
        if step == 5:
            end()
            each_head(pairs, span, mix)

    return work


def backward_beside(
    n,
    grad,
    mixed,
    gate,
    gain,
    q,
    k,
    v,
    running,
    logits,
    memory,
    g_gate,
    g_gain,
    g_q,
    g_k,
    g_v,
    g_logits,
    g_mixed,
    later,
    packed,
    held,
    sent,
    *sems,
):
    pairs = packed.shape[0]
    span = q.shape[0] // (pairs // HEADS)
    begin, carry, end = scan_steps(n, True, packed, later, held, sent, *sems)

    def gate_back(keys, values, state):
        gate_back_kernel(
            values(grad),
            values(mixed),
            values(gate),
            gain,
            keys(q),
            keys(running),
            values(g_gate),
            values(g_mixed),
            g_gain,
            state(packed),
        )

    def span_back(keys, values, state):
        span_back_kernel(
            keys(q),
            keys(k),
            values(v),
            keys(running),
            keys(logits),
            values(g_mixed),
            state(memory),
            state(later),
            keys(g_q),
            keys(g_k),
            values(g_v),
            keys(g_logits),
        )

    def work(step):
        if step == 0:
            g_gain[...] = jnp.zeros_like(g_gain)
            each_head(pairs, span, gate_back)
            begin()
        if step == 3:
            carry()
        if step == 5:
            end()
            each_head(pairs, span, span_back)

    return work


def matmul(left, right):
    return jnp.dot(left, right, preferred_element_type=jnp.float32)


def inner_rows(left, right):
    return lax.dot_general(
        left, right, (((0,), (0,)), ((), ())), preferred_element_type=jnp.float32
    )


def inner_low(left, right):
    return inner_rows(left, right).astype(jnp.bfloat16)


def times_transposed(left, right):
    return lax.dot_general(
        left, right, (((1,), (1,)), ((), ())), preferred_element_type=jnp.float32
    )


def rms_scale(source):
    return lax.rsqrt(jnp.mean(source * source, axis=-1, keepdims=True) + EPS)


def head_scale(source):
    return lax.rsqrt(jnp.maximum(jnp.mean(source * source, axis=-1, keepdims=True), 1.0))


def norm_back(grad_unit, unit, scale):
    return scale * (grad_unit - unit * jnp.mean(grad_unit * unit, axis=-1, keepdims=True))


def head_norm_back(grad_unit, unit, scale):
    live = jnp.where(scale < 1.0, 1.0, 0.0)
    return scale * (grad_unit - live * unit * jnp.mean(grad_unit * unit, axis=-1, keepdims=True))


def low_dot(left, right, left_axis=1, right_axis=0):
    return lax.dot_general(
        left.astype(jnp.bfloat16),
        right.astype(jnp.bfloat16),
        (((left_axis,), (right_axis,)), ((), ())),
        preferred_element_type=jnp.float32,
    )


def exact_sums(ones, source):
    total = jnp.zeros(source.shape, jnp.float32)
    for _ in range(3):
        high = source.astype(jnp.bfloat16)
        total = total + low_dot(ones, high)
        source = source - high.astype(jnp.float32)
    return total


def causal_mask(span):
    target = lax.broadcasted_iota(jnp.int32, (span, span), 0)
    source = lax.broadcasted_iota(jnp.int32, (span, span), 1)
    return target >= source


def pack(packed_ref, state, ending):
    width = state.shape[0]
    packed_ref[0, :width, :] = state.astype(jnp.bfloat16)
    tail = jnp.broadcast_to(jnp.exp(ending), (ROWS, ending.shape[1]))
    packed_ref[0, width:, :] = tail.astype(jnp.bfloat16)


def deposit_kernel(k_ref, v_ref, logits_ref, running_ref, packed_ref):
    logits = logits_ref[...]
    span = logits.shape[0]
    log_decay = (jnp.minimum(logits, 0.0) - jnp.log1p(jnp.exp(-jnp.abs(logits)))) / 16.0
    running = exact_sums(jnp.where(causal_mask(span), 1.0, 0.0), log_decay)
    running_ref[...] = running
    ending = running[span - 1 :, :]
    weighted = jnp.exp(ending - running) * k_ref[...].astype(jnp.float32)
    pack(packed_ref, low_dot(v_ref[...], weighted, 0, 0), ending)


def mix_kernel(q_ref, k_ref, v_ref, running_ref, memory_ref, gate_ref, gain_ref, mixed_ref, gated_ref):
    running = running_ref[...]
    span = running.shape[0]
    middle = running[span // 2 - 1 : span // 2, :]
    queries = q_ref[...].astype(jnp.float32) * KH ** (-0.5)
    rising = queries * jnp.exp(running - middle)
    falling = k_ref[...].astype(jnp.float32) * jnp.exp(middle - running)
    scores = jnp.where(causal_mask(span), low_dot(rising, falling, 1, 1), 0.0)
    mixed = low_dot(scores, v_ref[...])
    mixed = mixed + low_dot(queries * jnp.exp(running), memory_ref[0], 1, 1)
    mixed_ref[...] = mixed
    normed = mixed * head_scale(mixed) * gain_ref[...]
    gate = gate_ref[...]
    gated_ref[...] = (normed * gate * jax.nn.sigmoid(gate)).astype(jnp.bfloat16)


def gate_back_kernel(
    grad_ref, mixed_ref, gate_ref, gain_ref, q_ref, running_ref, gate_out_ref, g_ref, gain_out_ref, packed_ref
):
    grad, mixed, gate, gain = grad_ref[...], mixed_ref[...], gate_ref[...], gain_ref[...]
    scale = head_scale(mixed)
    unit = mixed * scale
    sig = jax.nn.sigmoid(gate)
    slope = sig * (1.0 + gate * (1.0 - sig))
    gate_out_ref[...] = (grad * unit * gain * slope).astype(jnp.bfloat16)
    grad_heads = grad * gate * sig

    gain_out_ref[...] += jnp.sum(grad_heads * unit, axis=0, keepdims=True)
    g_mixed = head_norm_back(grad_heads * gain, unit, scale).astype(jnp.bfloat16)
    g_ref[...] = g_mixed
    running = running_ref[...]
    span = running.shape[0]
    grown = q_ref[...].astype(jnp.float32) * KH ** (-0.5) * jnp.exp(running)
    pack(packed_ref, low_dot(g_mixed, grown, 0, 0), running[span - 1 :, :])


def span_back_kernel(
    q_ref, k_ref, v_ref, running_ref, logits_ref, g_ref, memory_ref, later_ref, gq_ref, gk_ref, gv_ref, gl_ref
):
    running, g, memory, later = running_ref[...], g_ref[...], memory_ref[0], later_ref[0]
    values = v_ref[...]
    span = running.shape[0]
    middle = running[span // 2 - 1 : span // 2, :]
    ending = running[span - 1 :, :]
    queries = q_ref[...].astype(jnp.float32) * KH ** (-0.5)
    key_rows = k_ref[...].astype(jnp.float32)
    grow, shrink = jnp.exp(running - middle), jnp.exp(middle - running)
    start, left = jnp.exp(running), jnp.exp(ending - running)
    rising = (queries * grow).astype(jnp.bfloat16)
    falling = (key_rows * shrink).astype(jnp.bfloat16)
    entered = (queries * start).astype(jnp.bfloat16)
    carried = (key_rows * left).astype(jnp.bfloat16)
    causal = causal_mask(span)
    scores = jnp.where(causal, low_dot(rising, falling, 1, 1), 0.0)
    g_scores = jnp.where(causal, low_dot(g, values, 1, 1), 0.0).astype(jnp.bfloat16)
    dq_within = low_dot(g_scores, falling)
    dk_within = low_dot(g_scores, rising, 0, 0)
    dq_across = low_dot(g, memory)
    dk_across = low_dot(values, later)
    gq_ref[...] = (KH ** (-0.5) * (grow * dq_within + start * dq_across)).astype(jnp.bfloat16)
    gk_ref[...] = (shrink * dk_within + left * dk_across).astype(jnp.bfloat16)
    gv_ref[...] = (low_dot(scores, g, 0, 0) + low_dot(carried, later, 1, 1)).astype(jnp.bfloat16)
    leaving = carried.astype(jnp.float32) * dk_across
    change = rising.astype(jnp.float32) * dq_within + entered.astype(jnp.float32) * dq_across
    change = change - falling.astype(jnp.float32) * dk_within - leaving
    kept = jnp.sum(memory.astype(jnp.float32) * later.astype(jnp.float32), axis=0, keepdims=True)
    at_end = jnp.sum(leaving, axis=0, keepdims=True) + jnp.exp(ending) * kept
    target = lax.broadcasted_iota(jnp.int32, (span, span), 0)
    source = lax.broadcasted_iota(jnp.int32, (span, span), 1)
    g_decay = exact_sums(jnp.where(source >= target, 1.0, 0.0), change) + at_end
    gl_ref[...] = g_decay * jax.nn.sigmoid(-logits_ref[...]) / 16.0


def forward(whole, inputs, ff_shards):
    (
        attn_gain,
        w_query,
        w_key,
        w_value,
        w_gate,
        w_rank_in,
        w_rank_out,
        rank_bias,
        out_gain,
        w_out,
        mlp_gain,
    ) = whole
    seqs, span, width = inputs.shape
    count = seqs * span
    rows_in = inputs.astype(jnp.float32).reshape(count, width)
    scale_in = rms_scale(rows_in)
    unit_in = rows_in * scale_in
    normed_in = (unit_in * attn_gain.astype(jnp.float32)).astype(jnp.bfloat16)
    queries = matmul(normed_in, w_query).astype(jnp.bfloat16)
    key_rows = matmul(normed_in, w_key).astype(jnp.bfloat16)
    values = matmul(normed_in, w_value).astype(jnp.bfloat16)
    gate_out = matmul(normed_in, w_gate)
    rank_rows = matmul(normed_in, w_rank_in)
    logits = jnp.dot(rank_rows, w_rank_out.astype(jnp.float32), precision=HIGH) + rank_bias.astype(
        jnp.float32
    )
    n = lax.axis_size("seq")
    pairs = seqs * HEADS
    up_pair, w_down, mixed, gated, running, memory_in = gather_all(
        ff_shards,
        1,
        forward_beside,
        (
            queries,
            key_rows,
            values,
            logits,
            gate_out,
            out_gain.astype(jnp.float32).reshape(1, VH),
        ),
        (
            jax.ShapeDtypeStruct((count, HEADS * VH), jnp.float32),
            jax.ShapeDtypeStruct((count, HEADS * VH), jnp.bfloat16),
            jax.ShapeDtypeStruct((count, HEADS * KH), jnp.float32),
            jax.ShapeDtypeStruct((pairs, VH, KH), jnp.bfloat16),
        ),
        scan_scratch(pairs, n),
    )
    hidden_width = up_pair.shape[1] // 2
    w_gate_ff, w_up = up_pair[:, :hidden_width], up_pair[:, hidden_width:]
    middle = rows_in + matmul(gated, w_out)
    scale_mid = rms_scale(middle)
    unit_mid = middle * scale_mid
    normed_mid = (unit_mid * mlp_gain.astype(jnp.float32)).astype(jnp.bfloat16)
    gate_ff = matmul(normed_mid, w_gate_ff)
    up_rows = matmul(normed_mid, w_up)
    hidden = (jax.nn.silu(gate_ff) * up_rows).astype(jnp.bfloat16)
    output = (middle + matmul(hidden, w_down)).astype(jnp.bfloat16).reshape(seqs, span, width)
    return (
        unit_in,
        scale_in,
        normed_in,
        queries,
        key_rows,
        values,
        running,
        memory_in,
        gate_out,
        rank_rows,
        logits,
        mixed,
        gated,
        unit_mid,
        scale_mid,
        normed_mid,
        gate_ff,
        up_rows,
        hidden,
        output,
        w_gate_ff,
        w_up,
        w_down,
    )


def backward(whole, kept, cotangent):
    (
        attn_gain,
        w_query,
        w_key,
        w_value,
        w_gate,
        w_rank_in,
        w_rank_out,
        rank_bias,
        out_gain,
        w_out,
        mlp_gain,
    ) = whole
    (
        unit_in,
        scale_in,
        normed_in,
        queries,
        key_rows,
        values,
        running,
        memory_in,
        gate_out,
        rank_rows,
        logits,
        mixed,
        gated,
        unit_mid,
        scale_mid,
        normed_mid,
        gate_ff,
        up_rows,
        hidden,
        output,
        w_gate_ff,
        w_up,
        w_down,
    ) = kept
    seqs, span, width = cotangent.shape
    count = seqs * span
    grad_rows = cotangent.reshape(count, width)
    grad_down = inner_low(hidden, grad_rows)
    grad_hidden = times_transposed(grad_rows, w_down)
    sig_ff = jax.nn.sigmoid(gate_ff)
    slope_ff = sig_ff * (1.0 + gate_ff * (1.0 - sig_ff))
    grad_gate_ff = (grad_hidden * up_rows * slope_ff).astype(jnp.bfloat16)
    grad_up_rows = (grad_hidden * gate_ff * sig_ff).astype(jnp.bfloat16)
    grad_pair_w = inner_low(normed_mid, jnp.concatenate([grad_gate_ff, grad_up_rows], axis=1))
    grad_normed_mid = times_transposed(grad_gate_ff, w_gate_ff) + times_transposed(
        grad_up_rows, w_up
    )
    grad_mlp_gain = jnp.sum(grad_normed_mid * unit_mid, axis=0)
    grad_middle = grad_rows.astype(jnp.float32) + norm_back(
        grad_normed_mid * mlp_gain.astype(jnp.float32), unit_mid, scale_mid
    )
    grad_branch = grad_middle.astype(jnp.bfloat16)
    grad_out_w = inner_low(gated, grad_branch)
    grad_gated = times_transposed(grad_branch, w_out)
    pairs = seqs * HEADS
    keys, vals = (count, HEADS * KH), (count, HEADS * VH)
    (
        grad_pair_w,
        grad_down,
        grad_gate_out,
        grad_out_gain,
        grad_queries,
        grad_keys,
        grad_values,
        grad_logits,
    ) = reduce_all(
        [grad_pair_w, grad_down],
        2,
        backward_beside,
        (
            grad_gated,
            mixed,
            gate_out,
            out_gain.astype(jnp.float32).reshape(1, VH),
            queries,
            key_rows,
            values,
            running,
            logits,
            memory_in,
        ),
        (
            jax.ShapeDtypeStruct(vals, jnp.bfloat16),
            jax.ShapeDtypeStruct((1, VH), jnp.float32),
            jax.ShapeDtypeStruct(keys, jnp.bfloat16),
            jax.ShapeDtypeStruct(keys, jnp.bfloat16),
            jax.ShapeDtypeStruct(vals, jnp.bfloat16),
            jax.ShapeDtypeStruct(keys, jnp.float32),
        ),
        (
            pltpu.VMEM(vals, jnp.bfloat16),
            pltpu.VMEM((pairs, VH, KH), jnp.bfloat16),
            *scan_scratch(pairs, lax.axis_size("seq")),
        ),
    )
    grad_bias = jnp.sum(grad_logits, axis=0)
    grad_rank_out = jnp.einsum("rq,rk->qk", rank_rows, grad_logits, precision=HIGH)
    grad_rank_rows = jnp.einsum(
        "rk,qk->rq", grad_logits, w_rank_out.astype(jnp.float32), precision=HIGH
    )
    grad_rank_in = jnp.einsum(
        "rd,rq->dq", normed_in.astype(jnp.float32), grad_rank_rows, precision=HIGH
    )
    grad_mixer_w = inner_low(
        normed_in, jnp.concatenate([grad_queries, grad_keys, grad_values, grad_gate_out], axis=1)
    )
    grad_normed_in = times_transposed(grad_queries, w_query) + times_transposed(grad_keys, w_key)
    grad_normed_in = (
        grad_normed_in
        + times_transposed(grad_values, w_value)
        + times_transposed(grad_gate_out, w_gate)
    )
    grad_normed_in = grad_normed_in + jnp.einsum(
        "rq,dq->rd", grad_rank_rows, w_rank_in.astype(jnp.float32), precision=HIGH
    )
    grad_attn_gain = jnp.sum(grad_normed_in * unit_in, axis=0)
    input_grad = grad_middle + norm_back(
        grad_normed_in * attn_gain.astype(jnp.float32), unit_in, scale_in
    )
    grads = (
        (grad_attn_gain, grad_rank_out, grad_bias, grad_out_gain, grad_mlp_gain),
        grad_mixer_w,
        grad_out_w,
        grad_rank_in,
        grad_pair_w,
        grad_down,
    )
    return (grads, input_grad.astype(jnp.bfloat16).reshape(seqs, span, width))


def body(
    inputs,
    cotangent,
    attn_gain,
    w_query,
    w_key,
    w_value,
    w_gate,
    w_rank_in,
    w_rank_out,
    rank_bias,
    out_gain,
    w_out,
    mlp_gain,
    w_gate_ff,
    w_up,
    w_down,
):
    n = lax.axis_size("seq")
    gains = (attn_gain, w_rank_out, rank_bias, out_gain, mlp_gain)
    rows = w_query.shape[0]
    flat = jnp.concatenate([gain.reshape(-1) for gain in gains])
    flat = jnp.pad(flat, (0, rows * SMALL - flat.size)).reshape(rows, SMALL)
    spare = jnp.zeros((rows, 128 - w_rank_in.shape[1] - SMALL), w_query.dtype)
    tail = jnp.concatenate([w_rank_in, flat, spare], axis=1)
    (mixer,) = gather_all([[w_query, w_key, w_value, w_gate, w_out, tail]], 0)
    cuts = [0]
    for weight in (w_query, w_key, w_value, w_gate, w_out, w_rank_in):
        cuts.append(cuts[-1] + weight.shape[1])
    parts = [mixer[:, low:high] for low, high in zip(cuts[:-1], cuts[1:])]
    flat = mixer[:, cuts[-1] : cuts[-1] + SMALL].reshape(n, rows * SMALL)
    small, at = [], 0
    for gain in gains:
        piece = flat[:, at : at + gain.size].reshape(n * gain.shape[0], *gain.shape[1:])
        small.append(piece)
        at += gain.size
    whole = (
        small[0],
        parts[0],
        parts[1],
        parts[2],
        parts[3],
        parts[5],
        small[1],
        small[2],
        small[3],
        parts[4],
        small[4],
    )
    kept = forward(whole, inputs, [[w_gate_ff, w_up], [w_down]])
    output = kept[-4]
    grads, input_grad = backward(whole, kept, cotangent)
    gain_grads, mixer, grad_out_w, grad_rank_in, up_pair, down = grads
    flat = jnp.concatenate(
        [grad.astype(jnp.bfloat16).reshape(n, -1) for grad in gain_grads], axis=1
    )
    flat = jnp.pad(flat, ((0, 0), (0, rows * SMALL - flat.shape[1]))).reshape(n * rows, SMALL)
    spare = jnp.zeros((n * rows, spare.shape[1]), jnp.bfloat16)
    rest = jnp.concatenate(
        [grad_out_w, grad_rank_in.astype(jnp.bfloat16), flat, spare], axis=1
    )
    mixer, rest = reduce_all([mixer, rest], 3)
    mixer = jnp.concatenate([mixer, rest], axis=1).astype(jnp.float32)
    up_pair = up_pair.astype(jnp.float32)
    parts = [mixer[:, start:end] for start, end in zip(cuts[:-1], cuts[1:])]
    flat = mixer[:, cuts[-1] : cuts[-1] + SMALL].reshape(-1)
    small, at = [], 0
    for gain in gains:
        small.append(flat[at : at + gain.size].reshape(gain.shape))
        at += gain.size
    summed = (
        small[0],
        parts[0],
        parts[1],
        parts[2],
        parts[3],
        parts[5],
        small[1],
        small[2],
        small[3],
        parts[4],
        small[4],
        up_pair[:, : w_gate_ff.shape[1]],
        up_pair[:, w_gate_ff.shape[1] :],
        down.astype(jnp.float32),
    )
    return (
        output,
        input_grad,
        summed[0],
        summed[1],
        summed[2],
        summed[3],
        summed[4],
        summed[5],
        summed[6],
        summed[7],
        summed[8],
        summed[9],
        summed[10],
        summed[11],
        summed[12],
        summed[13],
    )


def solution(mesh):
    placed = (
        P("dp", "seq", None),
        P("dp", "seq", None),
        P("seq"),
        P("seq", None),
        P("seq", None),
        P("seq", None),
        P("seq", None),
        P("seq", None),
        P("seq", None),
        P("seq"),
        P("seq"),
        P("seq", None),
        P("seq"),
        P("seq", None),
        P("seq", None),
        P("seq", None),
    )
    return jax.shard_map(
        body,
        mesh=mesh,
        in_specs=placed,
        out_specs=(
            P("dp", "seq", None),
            P("dp", "seq", None),
            P("seq"),
            P("seq", None),
            P("seq", None),
            P("seq", None),
            P("seq", None),
            P("seq", None),
            P("seq", None),
            P("seq"),
            P("seq"),
            P("seq", None),
            P("seq"),
            P("seq", None),
            P("seq", None),
            P("seq", None),
        ),
        check_vma=False,
    )
```
